32 devices in a mesh: groups: 2 (over y), row: 4 (over x, core), col: 4 (over z).
Axes of the slice: x: 2, y: 2, z: 4, core: 2. Of those that a mesh axis runs over, the one named last changes fastest.
Arguments:
- head_table: float32 [8192, 256], P(('groups', 'row', 'col')), parts along dimension 0, may hold values from -10 to 10, as said below
- head_accum: float32 [8192], P(('groups', 'row', 'col')), parts along dimension 0, may hold values from 0.1 to 2
- tail_table: float32 [8192, 256], P(('groups', 'row', 'col')), parts along dimension 0, may hold values from -10 to 10, as said below
- tail_accum: float32 [8192], P(('groups', 'row', 'col')), parts along dimension 0, may hold values from 0.1 to 2
- relations: float32 [2048, 256], P('groups'), parts along dimension 0, may hold values from -1.5 to 1.5
- relation_accum: float32 [2048], P('groups'), parts along dimension 0, may hold values from 0.1 to 2
- head_rows: int32 [32, 2, 1024], P(('groups', 'row', 'col')), parts along dimension 0, may hold values from 0 to 255
- tail_rows: int32 [32, 2, 1024], P(('groups', 'row', 'col')), parts along dimension 0, may hold values from 0 to 255
- relation_ids: int32 [32, 2, 1024], P(('groups', 'row', 'col')), parts along dimension 0, may hold values from 0 to 1023
- negative_rows: int32 [32, 2, 256], P(('groups', 'row', 'col')), parts along dimension 0, may hold values from 0 to 255
Outputs:
- head_table_out: float32 [8192, 256], P(('groups', 'row', 'col')), parts along dimension 0
- head_accum_out: float32 [8192], P(('groups', 'row', 'col')), parts along dimension 0
- tail_table_out: float32 [8192, 256], P(('groups', 'row', 'col')), parts along dimension 0
- tail_accum_out: float32 [8192], P(('groups', 'row', 'col')), parts along dimension 0
- relations_out: float32 [2048, 256], P('groups'), parts along dimension 0
- relation_accum_out: float32 [2048], P('groups'), parts along dimension 0
The draws below stay inside these ranges and needn't reach their ends.
There are 2 independent parts, one for each index of `groups`. The reference program is written for one: setup_inputs(seed, part) draws one part's arguments, and reference() takes and returns one part's arrays. A program takes and returns all parts, laid end to end along the dimension named above; each array names one. Nothing has to cross between parts.
Inputs may be any that keep to these rules, and one draw needn't show every extreme that they name: `head_table`: embedding rows of independent entries with row scales that differ. `tail_table`: embedding rows of independent entries with row scales that differ.
All inputs are finite; a program needn't handle non-finite values.
Results may differ from the reference program's by a relative error of at most 0.0003.
Values sent between devices are 32-bit elements; how exact they have to be, the bound alone decides.
A program may use at most 64 MiB of HBM per device.

```python
import math
import jax
import jax.numpy as jnp
import numpy as np
from jax import lax

D = 256
NREL = 1024
NNEG = 256
BUCKETS = 2
ROWS = 256
EDGES = 1024
BLOCKS = 16
ENTITIES = 4096
N_ROW = 4
N_COL = 4


def draw_head_table(key, part):
    key = jax.random.fold_in(key, 11)
    value_key, scale_key = jax.random.split(key)
    values = jnp.clip(jax.random.normal(value_key, (ENTITIES, D), jnp.float32), -6.0, 6.0)
    scales = jnp.exp(jax.random.uniform(scale_key, (ENTITIES, 1), jnp.float32, math.log(0.2), math.log(0.6)))
    return values * scales


def draw_tail_table(key, part):
    key = jax.random.fold_in(key, 23)
    value_key, scale_key = jax.random.split(key)
    values = jnp.clip(jax.random.normal(value_key, (ENTITIES, D), jnp.float32), -6.0, 6.0)
    scales = jnp.exp(jax.random.uniform(scale_key, (ENTITIES, 1), jnp.float32, math.log(0.2), math.log(0.6)))
    return values * scales


def touch_ends(drawn, key, low, top_value):
    extent = drawn.shape
    place = [jax.random.randint(jax.random.fold_in(key, axis), (), 0, extent[axis]) for axis in range(len(extent))]
    drawn = drawn.at[tuple(place)].set(low)
    longest = extent.index(max(extent))
    place[longest] = (place[longest] + 1) % extent[longest]
    return drawn.at[tuple(place)].set(top_value)


def block_levels(stream_key, dims, cuts, smallest, top_value):
    factor_of, own = 1.0, jax.random.fold_in(stream_key, 6)
    for dim, parts in cuts:
        draws = jnp.exp(jax.random.uniform(jax.random.fold_in(own, dim), (parts,), jnp.float32, smallest / len(cuts), top_value / len(cuts)))
        factor_of = factor_of * jnp.repeat(draws, dims[dim] // parts).reshape([-1 if axis == dim else 1 for axis in range(len(dims))])
    return factor_of


def cumulative_ranks(count, skew):
    weights = [(1 << 20) // math.isqrt(rank ** skew) + 1 for rank in range(1, count + 1)]
    deviation = 1 + sum(weights) // (1 << 30)
    return np.cumsum(np.array([max(1, weight // deviation) for weight in weights]))


def ranked_ids(own_key, extent, count, lean):
    grid = cumulative_ranks(count, lean)
    lot = jax.random.randint(jax.random.fold_in(own_key, 1), extent, 0, int(grid[count - 1]))
    standing = jnp.searchsorted(jnp.asarray(grid, jnp.int32), lot, side="right")
    return jax.random.permutation(jax.random.fold_in(own_key, 2), count)[standing].astype(jnp.int32)


def setup_inputs(seed: int = 0, part: int = 0) -> dict:
    key_list = jax.random.split(jax.random.key(seed), 11)
    own_keys = jax.random.split(jax.random.fold_in(key_list[10], part), 11)
    head_table = draw_head_table(jax.random.fold_in(jax.random.fold_in(key_list[10], part), 71), part)
    head_accum = jnp.clip(jnp.exp(math.log(2.0) - 2.9957323 * jax.random.uniform(own_keys[1], (ENTITIES,), jnp.float32) ** block_levels(own_keys[1], (ENTITIES,), ((0, 16),), -0.2, 0.2)), 0.1, 2.0)
    tail_table = draw_tail_table(jax.random.fold_in(jax.random.fold_in(key_list[10], part), 71), part)
    tail_accum = jnp.clip(jnp.exp(math.log(2.0) - 2.9957323 * jax.random.uniform(own_keys[3], (ENTITIES,), jnp.float32) ** block_levels(own_keys[3], (ENTITIES,), ((0, 16),), -0.2, 0.2)), 0.1, 2.0)
    relations = jnp.clip(jax.random.uniform(own_keys[4], (NREL, D), jnp.float32, -1.5, 1.5), -1.5, 1.5)
    relation_accum = jnp.clip(jnp.exp(jax.random.uniform(own_keys[5], (NREL,), jnp.float32, math.log(0.1), math.log(2.0))), 0.1, 2.0)
    head_rows = touch_ends(jax.random.randint(own_keys[6], (BLOCKS, BUCKETS, EDGES), 0, ROWS), jax.random.fold_in(own_keys[6], 1), 0, ROWS - 1).astype(jnp.int32)
    tail_rows = touch_ends(jax.random.randint(own_keys[7], (BLOCKS, BUCKETS, EDGES), 0, ROWS), jax.random.fold_in(own_keys[7], 1), 0, ROWS - 1).astype(jnp.int32)
    relation_ids = touch_ends(ranked_ids(own_keys[8], (BLOCKS, BUCKETS, EDGES), NREL, 2), jax.random.fold_in(own_keys[8], 3), 0, NREL - 1).astype(jnp.int32)
    negative_rows = touch_ends(jax.random.randint(own_keys[9], (BLOCKS, BUCKETS, NNEG), 0, ROWS), jax.random.fold_in(own_keys[9], 1), 0, ROWS - 1).astype(jnp.int32)
    return dict(head_table=head_table, head_accum=head_accum, tail_table=tail_table, tail_accum=tail_accum, relations=relations, relation_accum=relation_accum, head_rows=head_rows, tail_rows=tail_rows, relation_ids=relation_ids, negative_rows=negative_rows)


learn_rate = 0.1

def edge_terms(head_block, tail_block, relations, head_sel, rel_sel, tail_sel, neg_sel):
    rows_here = head_block.shape[0]
    heads_e = jnp.take(head_block, head_sel, axis=0)
    rels_e = jnp.take(relations, rel_sel, axis=0)
    tails_e = jnp.take(tail_block, tail_sel, axis=0)
    negatives = jnp.take(tail_block, neg_sel, axis=0)
    head_rel = heads_e * rels_e
    positive = lax.optimization_barrier(jnp.sum(head_rel * tails_e, axis=1))
    scores = jnp.einsum('ed,nd->en', head_rel, negatives, precision=lax.Precision.HIGHEST)
    ceiling = jnp.maximum(positive, lax.optimization_barrier(jnp.max(scores, axis=1)))
    pos_weight = jnp.exp(positive - ceiling)
    neg_weight = jnp.exp(scores - ceiling[:, None])
    denominator = pos_weight + lax.optimization_barrier(jnp.sum(neg_weight, axis=1))
    pos_grad = pos_weight / denominator - 1.0
    neg_grad = neg_weight / denominator[:, None]
    grad_pair = pos_grad[:, None] * tails_e + jnp.dot(neg_grad, negatives, precision=lax.Precision.HIGHEST)
    grad_head = jax.ops.segment_sum(grad_pair * rels_e, head_sel, num_segments=rows_here)
    grad_rel = jax.ops.segment_sum(grad_pair * heads_e, rel_sel, num_segments=relations.shape[0])
    grad_negs = jnp.einsum('en,ed->nd', neg_grad, head_rel, precision=lax.Precision.HIGHEST)
    grad_tail = jax.ops.segment_sum(pos_grad[:, None] * head_rel, tail_sel, num_segments=rows_here)
    grad_tail = grad_tail + jax.ops.segment_sum(grad_negs, neg_sel, num_segments=rows_here)
    return (grad_head, grad_tail, grad_rel)

def bucket_grads(head_block, tail_block, relations, head_sel, rel_sel, tail_sel, neg_sel):
    edge_total = head_sel.shape[0]
    block_len = min(edge_total, 1024)
    block_count = edge_total // block_len

    def accumulate(block_index, running):
        block_start = block_index * block_len
        head_part = lax.dynamic_slice_in_dim(head_sel, block_start, block_len)
        rel_part = lax.dynamic_slice_in_dim(rel_sel, block_start, block_len)
        tail_part = lax.dynamic_slice_in_dim(tail_sel, block_start, block_len)
        terms = edge_terms(head_block, tail_block, relations, head_part, rel_part, tail_part, neg_sel)
        return (running[0] + terms[0], running[1] + terms[1], running[2] + terms[2])
    start_sums = (jnp.zeros(head_block.shape, jnp.float32), jnp.zeros(tail_block.shape, jnp.float32), jnp.zeros(relations.shape, jnp.float32))
    return lax.fori_loop(0, block_count, accumulate, start_sums)

def adagrad_rows(weights, accumulator, gradient):
    updated = accumulator + lax.optimization_barrier(jnp.mean(gradient * gradient, axis=1))
    return (weights - learn_rate * gradient / jnp.sqrt(updated)[:, None], updated)

def run_bucket(head_blocks, head_accs, tail_blocks, tail_accs, relations, head_sel, rel_sel, tail_sel, neg_sel):

    def visit(rel_running, inputs):
        head_block, head_acc, tail_block, tail_acc, head_ids, rel_ids, tail_ids, neg_ids = inputs
        grad_head, grad_tail, grad_rel = bucket_grads(head_block, tail_block, relations, head_ids, rel_ids, tail_ids, neg_ids)
        new_head, new_head_acc = adagrad_rows(head_block, head_acc, grad_head)
        new_tail, new_tail_acc = adagrad_rows(tail_block, tail_acc, grad_tail)
        return (rel_running + grad_rel, (new_head, new_head_acc, new_tail, new_tail_acc))
    rel_start = jnp.zeros(relations.shape, jnp.float32)
    return lax.scan(visit, rel_start, (head_blocks, head_accs, tail_blocks, tail_accs, head_sel, rel_sel, tail_sel, neg_sel))

def reference(head_table, head_accum, tail_table, tail_accum, relations, relation_accum, head_rows, tail_rows, relation_ids, negative_rows):
    head_blocks = head_table.reshape(BLOCKS, ROWS, D)
    tail_blocks = tail_table.reshape(BLOCKS, ROWS, D)
    head_accs = head_accum.reshape(BLOCKS, ROWS)
    tail_accs = tail_accum.reshape(BLOCKS, ROWS)
    rel_one, outcome = run_bucket(head_blocks, head_accs, tail_blocks, tail_accs, relations, head_rows[:, 0], relation_ids[:, 0], tail_rows[:, 0], negative_rows[:, 0])
    head_blocks, head_accs, tail_blocks, tail_accs = outcome
    head_blocks = jnp.roll(head_blocks.reshape(N_ROW, N_COL, ROWS, D), 1, axis=0).reshape(BLOCKS, ROWS, D)
    head_accs = jnp.roll(head_accs.reshape(N_ROW, N_COL, ROWS), 1, axis=0).reshape(BLOCKS, ROWS)
    tail_blocks = jnp.roll(tail_blocks.reshape(N_ROW, N_COL, ROWS, D), 1, axis=1).reshape(BLOCKS, ROWS, D)
    tail_accs = jnp.roll(tail_accs.reshape(N_ROW, N_COL, ROWS), 1, axis=1).reshape(BLOCKS, ROWS)
    rel_two, outcome = run_bucket(head_blocks, head_accs, tail_blocks, tail_accs, relations, head_rows[:, 1], relation_ids[:, 1], tail_rows[:, 1], negative_rows[:, 1])
    head_blocks, head_accs, tail_blocks, tail_accs = outcome
    relations_out, relation_accum_out = adagrad_rows(relations, relation_accum, rel_one + rel_two)
    return (head_blocks.reshape(ENTITIES, D), head_accs.reshape(ENTITIES), tail_blocks.reshape(ENTITIES, D), tail_accs.reshape(ENTITIES), relations_out, relation_accum_out)
```

```python
import functools

import jax
import jax.numpy as jnp
from jax import lax
from jax.experimental import pallas as pl
from jax.experimental.pallas import tpu as pltpu
from jax.sharding import PartitionSpec as P

learn_rate = 0.1
edge_tile = 256
f32 = jnp.float32
bf16 = jnp.bfloat16
MESH = pl.DeviceIdType.MESH


def split(value):
    high = value.astype(bf16)
    return high, (value - high.astype(f32)).astype(bf16)


def dot(a, b):
    return jnp.dot(a, b, preferred_element_type=f32)


def dot_nt(a, b):
    return lax.dot_general(a, b, (((1,), (1,)), ((), ())), preferred_element_type=f32)


def onehot(ids, count):
    rows = lax.broadcasted_iota(jnp.int32, (count, ids.shape[1]), 0)
    return rows == ids


def column(row):
    wide = jnp.broadcast_to(row, (128, row.shape[1]))
    return jnp.transpose(wide)[:, :1]


def as_row(col):
    wide = jnp.broadcast_to(col, (col.shape[0], 128))
    return jnp.transpose(wide)[:8]


def adagrad(weights, accum_row, gradient):
    width = gradient.shape[1]
    mean = jnp.sum(gradient * gradient, axis=1, keepdims=True) * (1.0 / width)
    updated = column(accum_row) + mean
    return weights - gradient * (learn_rate / jnp.sqrt(updated)), as_row(updated)


def kernel(
    n_row,
    n_col,
    head_ref,
    head_acc_ref,
    tail_ref,
    tail_acc_ref,
    rel_ref,
    rel_acc_ref,
    head_ids,
    tail_ids,
    rel_ids,
    neg_ids,
    head_out,
    head_acc_out,
    tail_out,
    tail_acc_out,
    rel_out,
    rel_acc_out,
    rel_t,
    rel_hot,
    rels_e,
    heads_e,
    hq_hi,
    hq_lo,
    wt_hi,
    wt_lo,
    by_head_hi,
    by_head_lo,
    by_rel_hi,
    by_rel_lo,
    head_send,
    tail_send,
    head_in,
    tail_in,
    grad,
    core_in,
    x_in,
    z_in,
    total,
    move_send,
    move_recv,
    core_send,
    core_recv,
    xs_send,
    xs_recv,
    zs_send,
    zs_recv,
    zg_send,
    zg_recv,
    xg_send,
    xg_recv,
    cg_send,
    cg_recv,
):
    n_x = n_row // 2
    rows, width = head_ref.shape
    n_rel = rel_ref.shape[0]
    edges = head_ids.shape[1]
    half = width // 2
    x_rows = n_rel // n_x
    z_rows = x_rows // n_col
    r = lax.axis_index("row")
    c = lax.axis_index("col")
    x = lax.div(r, 2)
    h = lax.rem(r, 2)
    sibling = x * 2 + (1 - h)

    barrier = pltpu.get_barrier_semaphore()
    for k in range(1, n_row):
        pl.semaphore_signal(barrier, inc=1, device_id={"row": lax.rem(r + k, n_row)}, device_id_type=MESH)
    for k in range(1, n_col):
        pl.semaphore_signal(barrier, inc=1, device_id={"col": lax.rem(c + k, n_col)}, device_id_type=MESH)

    def remote(src, dst, send, recv, device):
        return pltpu.make_async_remote_copy(
            src_ref=src, dst_ref=dst, send_sem=send, recv_sem=recv, device_id=device, device_id_type=MESH
        )

    def gather_rels(b):
        for e0 in range(0, edges, edge_tile):
            cols = slice(e0, e0 + edge_tile)
            hot = onehot(rel_ids[b : b + 1, cols], n_rel).astype(bf16)
            rel_hot[b, :, cols] = hot
            both = dot(rel_t[...], hot)
            rels_e[b, :, cols] = both[:width] + both[width:]

    def weigh(b, head, tail):
        head_t = jnp.concatenate(split(jnp.transpose(head)), axis=0)
        tail_hi, tail_lo = split(tail)
        tail_both = jnp.concatenate([tail_hi, tail_lo], axis=0)
        counts = jnp.sum(onehot(neg_ids[b : b + 1, :], rows).astype(f32), axis=1, keepdims=True)
        for e0 in range(0, edges, edge_tile):
            cols = slice(e0, e0 + edge_tile)
            both = dot(head_t, onehot(head_ids[b : b + 1, cols], rows).astype(bf16))
            heads = both[:rows] + both[rows:]
            heads_e[:, cols] = heads
            hi, lo = split(heads * rels_e[b, :, cols])
            hq_hi[:, cols] = hi
            hq_lo[:, cols] = lo
            both = dot(tail_both, hi)
            scores = both[:rows] + both[rows:] + dot(tail_hi, lo)
            tail_hot = onehot(tail_ids[b : b + 1, cols], rows)
            positive = jnp.sum(jnp.where(tail_hot, scores, 0.0), axis=0, keepdims=True)
            scores = jnp.where(counts > 0.0, scores, -3e38)
            ceiling = jnp.maximum(jnp.max(scores, axis=0, keepdims=True), positive)
            pos_exp = jnp.exp(positive - ceiling)
            neg_exp = jnp.exp(scores - ceiling) * counts
            inverse = 1.0 / (pos_exp + jnp.sum(neg_exp, axis=0, keepdims=True))
            weight = neg_exp * inverse + jnp.where(tail_hot, pos_exp * inverse - 1.0, 0.0)
            hi, lo = split(weight)
            wt_hi[:, cols] = hi
            wt_lo[:, cols] = lo

    def tail_gradient():
        return dot_nt(wt_hi[...], hq_hi[...]) + dot_nt(wt_hi[...], hq_lo[...]) + dot_nt(wt_lo[...], hq_hi[...])

    def pair_gradients(b, tail):
        tail_t_hi, tail_t_lo = split(jnp.transpose(tail))
        tail_t = jnp.concatenate([tail_t_hi, tail_t_lo], axis=0)
        for e0 in range(0, edges, edge_tile):
            cols = slice(e0, e0 + edge_tile)
            both = dot(tail_t, wt_hi[:, cols])
            pair = both[:width] + both[width:] + dot(tail_t_hi, wt_lo[:, cols])
            hi, lo = split(pair * rels_e[b, :, cols])
            by_head_hi[:, cols] = hi
            by_head_lo[:, cols] = lo
            hi, lo = split(pair * heads_e[:, cols])
            by_rel_hi[:, cols] = hi
            by_rel_lo[:, cols] = lo

    def head_gradient(b):
        hot = onehot(head_ids[b : b + 1, :], rows).astype(bf16)
        return dot_nt(hot, by_head_hi[...]) + dot_nt(hot, by_head_lo[...])

    rel_t[...] = jnp.concatenate(split(jnp.transpose(rel_ref[...])), axis=0)
    gather_rels(0)
    weigh(0, head_ref[...], tail_ref[...])
    tail_new, tail_acc_new = adagrad(tail_ref[...], tail_acc_ref[...], tail_gradient())
    tail_send[:rows] = tail_new
    tail_send[rows:] = tail_acc_new
    pl.semaphore_wait(barrier, n_row + n_col - 2)
    tail_move = remote(tail_send, tail_in, move_send.at[0], move_recv.at[0], {"col": lax.rem(c + 1, n_col)})
    tail_move.start()
    pair_gradients(0, tail_ref[...])
    head_new, head_acc_new = adagrad(head_ref[...], head_acc_ref[...], head_gradient(0))
    head_send[:rows] = head_new
    head_send[rows:] = head_acc_new
    head_move = remote(head_send, head_in, move_send.at[1], move_recv.at[1], {"row": lax.rem(r + 1, n_row)})
    head_move.start()
    rel_one = dot_nt(rel_hot[0], by_rel_hi[...]) + dot_nt(rel_hot[0], by_rel_lo[...])
    grad[0] = rel_one[:, :half]
    grad[1] = rel_one[:, half:]
    gather_rels(1)
    head_move.wait()
    tail_move.wait()

    weigh(1, head_in[:rows], tail_in[:rows])
    pair_gradients(1, tail_in[:rows])

    def x_start(i):
        return pl.multiple_of(lax.rem(x + i, n_x) * x_rows, x_rows)

    def z_start(i, k):
        return pl.multiple_of((lax.rem(x + i, n_x) * n_col + lax.rem(c + k, n_col)) * z_rows, z_rows)

    x_order = list(range(1, n_x)) + [0]
    z_order = list(range(1, n_col)) + [0]
    core_moves = {}
    for i in x_order:
        here = pl.ds(x_start(i), x_rows)
        part = dot_nt(rel_hot[1, here], by_rel_hi[...]) + dot_nt(rel_hot[1, here], by_rel_lo[...])
        grad[0, here] = grad[0, here] + part[:, :half]
        grad[1, here] = grad[1, here] + part[:, half:]
        core_moves[i] = remote(
            grad.at[1 - h, here], core_in.at[here], core_send.at[i], core_recv.at[i], {"row": sibling}
        )
        core_moves[i].start()

    x_moves = {}
    for i in x_order:
        core_moves[i].wait_recv()
        for k in z_order:
            here = pl.ds(z_start(i, k), z_rows)
            grad[h, here] = grad[h, here] + core_in[here]
            if i:
                slot = (i - 1) * n_col + k
                x_moves[i, k] = remote(
                    grad.at[h, here],
                    x_in.at[slot],
                    xs_send.at[slot],
                    xs_recv.at[slot],
                    {"row": lax.rem(x + i, n_x) * 2 + h},
                )
                x_moves[i, k].start()

    head_final, head_acc_final = adagrad(head_in[:rows], head_in[rows : rows + 1], head_gradient(1))
    head_out[...] = head_final
    head_acc_out[...] = head_acc_final[:1]
    tail_final, tail_acc_final = adagrad(tail_in[:rows], tail_in[rows : rows + 1], tail_gradient())
    tail_out[...] = tail_final
    tail_acc_out[...] = tail_acc_final[:1]

    z_moves = {}
    for k in z_order:
        here = pl.ds(z_start(0, k), z_rows)
        value = grad[h, here]
        for i in range(1, n_x):
            x_moves[i, k].wait_recv()
            value = value + x_in[(i - 1) * n_col + k]
        grad[h, here] = value
        if k:
            z_moves[k] = remote(
                grad.at[h, here],
                z_in.at[k - 1],
                zs_send.at[k - 1],
                zs_recv.at[k - 1],
                {"col": lax.rem(c + k, n_col)},
            )
            z_moves[k].start()

    mine = pl.ds(z_start(0, 0), z_rows)
    value = grad[h, mine]
    for k in range(1, n_col):
        z_moves[k].wait_recv()
        value = value + z_in[k - 1]
    total[h, mine] = value

    gathers = []

    def spread(slot_x, slot_z, to_x):
        piece = total.at[h, pl.ds(z_start(slot_x, slot_z), z_rows)]
        if to_x:
            for i in range(1, n_x):
                slot = (i - 1) * n_col + slot_z
                gathers.append(
                    remote(piece, piece, xg_send.at[slot], xg_recv.at[slot], {"row": lax.rem(x + i, n_x) * 2 + h})
                )
                gathers[-1].start()
        slot = slot_x * n_col + slot_z
        gathers.append(remote(piece, piece, cg_send.at[slot], cg_recv.at[slot], {"row": sibling}))
        gathers[-1].start()

    piece = total.at[h, mine]
    for k in range(1, n_col):
        gathers.append(
            remote(piece, piece, zg_send.at[k - 1], zg_recv.at[k - 1], {"col": lax.rem(c + k, n_col)})
        )
        gathers[-1].start()
    spread(0, 0, True)

    def arrived(piece, sem):
        pltpu.make_async_copy(piece, piece, sem).wait()

    for k in range(1, n_col):
        from_z = n_col - k
        arrived(total.at[h, pl.ds(z_start(0, from_z), z_rows)], zg_recv.at[k - 1])
        spread(0, from_z, True)
    for k in [0] + list(range(n_col - 1, 0, -1)):
        for i in range(1, n_x):
            from_x = n_x - i
            arrived(total.at[h, pl.ds(z_start(from_x, k), z_rows)], xg_recv.at[(i - 1) * n_col + k])
            spread(from_x, k, False)
    for i in range(n_x):
        for k in range(n_col):
            arrived(total.at[1 - h, pl.ds(z_start(i, k), z_rows)], cg_recv.at[i * n_col + k])

    for r0 in range(0, n_rel, rows):
        here = slice(r0, r0 + rows)
        both = jnp.concatenate([total[0, here], total[1, here]], axis=1)
        rel_new, rel_acc_new = adagrad(rel_ref[here], rel_acc_ref[:, here], both)
        rel_out[here] = rel_new
        rel_acc_out[:, here] = rel_acc_new[:1]

    for move in list(core_moves.values()) + list(x_moves.values()) + list(z_moves.values()) + gathers:
        move.wait_send()


def shards(
    n_row,
    n_col,
    head_table,
    head_accum,
    tail_table,
    tail_accum,
    relations,
    relation_accum,
    head_rows,
    tail_rows,
    relation_ids,
    negative_rows,
):
    rows, width = head_table.shape
    n_rel = relations.shape[0]
    buckets, edges = head_rows.shape[1:]
    n_x = n_row // 2
    half = width // 2
    z_rows = n_rel // (n_x * n_col)
    shape = jax.ShapeDtypeStruct
    vmem = pl.BlockSpec(memory_space=pltpu.VMEM)
    dma = pltpu.SemaphoreType.DMA
    x_slots = max(1, (n_x - 1) * n_col)
    z_slots = max(1, n_col - 1)
    edge_piece = pltpu.VMEM((width, edges), bf16)
    moved = pltpu.VMEM((rows + 8, width), f32)
    outs = pl.pallas_call(
        functools.partial(kernel, n_row, n_col),
        out_shape=(
            shape((rows, width), f32),
            shape((1, rows), f32),
            shape((rows, width), f32),
            shape((1, rows), f32),
            shape((n_rel, width), f32),
            shape((1, n_rel), f32),
        ),
        in_specs=[vmem] * 10,
        out_specs=(vmem,) * 6,
        scratch_shapes=[
            pltpu.VMEM((2 * width, n_rel), bf16),
            pltpu.VMEM((buckets, n_rel, edges), bf16),
            pltpu.VMEM((buckets, width, edges), f32),
            pltpu.VMEM((width, edges), f32),
            edge_piece,
            edge_piece,
            pltpu.VMEM((rows, edges), bf16),
            pltpu.VMEM((rows, edges), bf16),
            edge_piece,
            edge_piece,
            edge_piece,
            edge_piece,
            moved,
            moved,
            moved,
            moved,
            pltpu.VMEM((2, n_rel, half), f32),
            pltpu.VMEM((n_rel, half), f32),
            pltpu.VMEM((x_slots, z_rows, half), f32),
            pltpu.VMEM((z_slots, z_rows, half), f32),
            pltpu.VMEM((2, n_rel, half), f32),
            dma((2,)),
            dma((2,)),
            dma((n_x,)),
            dma((n_x,)),
            dma((x_slots,)),
            dma((x_slots,)),
            dma((z_slots,)),
            dma((z_slots,)),
            dma((z_slots,)),
            dma((z_slots,)),
            dma((x_slots,)),
            dma((x_slots,)),
            dma((n_x * n_col,)),
            dma((n_x * n_col,)),
        ],
        compiler_params=pltpu.CompilerParams(
            collective_id=0, has_side_effects=True, vmem_limit_bytes=50 * 2**20
        ),
    )(
        head_table,
        head_accum.reshape(1, rows),
        tail_table,
        tail_accum.reshape(1, rows),
        relations,
        relation_accum.reshape(1, n_rel),
        head_rows[0],
        tail_rows[0],
        relation_ids[0],
        negative_rows[0],
    )
    return (outs[0], outs[1][0], outs[2], outs[3][0], outs[4], outs[5][0])


def solution(mesh):
    block = P(("groups", "row", "col"))
    return jax.shard_map(
        functools.partial(shards, mesh.shape["row"], mesh.shape["col"]),
        mesh=mesh,
        in_specs=(block, block, block, block, P("groups"), P("groups"), block, block, block, block),
        out_specs=(block, block, block, block, P("groups"), P("groups")),
        check_vma=False,
    )
```

```python
import functools

import jax
import jax.numpy as jnp
from jax import lax
from jax.experimental import pallas as pl
from jax.experimental.pallas import tpu as pltpu
from jax.sharding import PartitionSpec as P

learn_rate = 0.1
edge_tile = 256
f32 = jnp.float32
bf16 = jnp.bfloat16
MESH = pl.DeviceIdType.MESH


def split(value):
    high = value.astype(bf16)
    return high, (value - high.astype(f32)).astype(bf16)


def dot(a, b):
    return jnp.dot(a, b, preferred_element_type=f32)


def dot_nt(a, b):
    return lax.dot_general(a, b, (((1,), (1,)), ((), ())), preferred_element_type=f32)


def onehot(ids, count):
    rows = lax.broadcasted_iota(jnp.int32, (count, ids.shape[1]), 0)
    return rows == ids


def column(row):
    wide = jnp.broadcast_to(row, (128, row.shape[1]))
    return jnp.transpose(wide)[:, :1]


def as_row(col):
    wide = jnp.broadcast_to(col, (col.shape[0], 128))
    return jnp.transpose(wide)[:8]


def adagrad(weights, accum_row, gradient):
    width = gradient.shape[1]
    mean = jnp.sum(gradient * gradient, axis=1, keepdims=True) * (1.0 / width)
    updated = column(accum_row) + mean
    return weights - gradient * (learn_rate / jnp.sqrt(updated)), as_row(updated)


def kernel(
    n_row,
    n_col,
    head_hbm,
    head_acc_hbm,
    tail_hbm,
    tail_acc_hbm,
    rel_hbm,
    rel_acc_hbm,
    head_ids_hbm,
    tail_ids_hbm,
    rel_ids_hbm,
    neg_ids_hbm,
    head_out_hbm,
    head_acc_out_hbm,
    tail_out_hbm,
    tail_acc_out_hbm,
    rel_out_hbm,
    rel_acc_out_hbm,
    head_ref,
    head_acc_ref,
    tail_ref,
    tail_acc_ref,
    rel_ref,
    rel_acc_ref,
    head_ids,
    tail_ids,
    rel_ids,
    neg_ids,
    load_sems,
    head_out,
    head_acc_out,
    tail_out,
    tail_acc_out,
    rel_out,
    rel_acc_out,
    rel_acc_wide,
    store_sems,
    rel_store_sems,
    rel_t,
    rel_hot,
    rels_e,
    heads_e,
    hq_hi,
    hq_lo,
    wt_hi,
    wt_lo,
    by_head_hi,
    by_head_lo,
    by_rel_hi,
    by_rel_lo,
    head_send,
    tail_send,
    head_in,
    tail_in,
    grad,
    core_in,
    x_in,
    z_in,
    total,
    move_send,
    move_recv,
    core_send,
    core_recv,
    xs_send,
    xs_recv,
    zs_send,
    zs_recv,
    zg_send,
    zg_recv,
    xg_send,
    xg_recv,
    cg_send,
    cg_recv,
):
    n_x = n_row // 2
    rows, width = head_ref.shape
    n_rel = rel_ref.shape[0]
    edges = head_ids.shape[1]
    half = width // 2
    x_rows = n_rel // n_x
    z_rows = x_rows // n_col
    r = lax.axis_index("row")
    c = lax.axis_index("col")
    x = lax.div(r, 2)
    h = lax.rem(r, 2)
    sibling = x * 2 + (1 - h)

    pairs = (
        (rel_hbm, rel_ref),
        (rel_ids_hbm, rel_ids),
        (head_hbm, head_ref),
        (head_ids_hbm, head_ids),
        (tail_hbm, tail_ref),
        (tail_ids_hbm, tail_ids),
        (neg_ids_hbm, neg_ids),
        (tail_acc_hbm, tail_acc_ref),
        (head_acc_hbm, head_acc_ref),
        (rel_acc_hbm, rel_acc_ref),
    )
    loads = [pltpu.make_async_copy(src, dst, load_sems.at[n]) for n, (src, dst) in enumerate(pairs)]
    for load in loads:
        load.start()

    barrier = pltpu.get_barrier_semaphore()
    for k in range(1, n_row):
        pl.semaphore_signal(barrier, inc=1, device_id={"row": lax.rem(r + k, n_row)}, device_id_type=MESH)
    for k in range(1, n_col):
        pl.semaphore_signal(barrier, inc=1, device_id={"col": lax.rem(c + k, n_col)}, device_id_type=MESH)

    def remote(src, dst, send, recv, device):
        return pltpu.make_async_remote_copy(
            src_ref=src, dst_ref=dst, send_sem=send, recv_sem=recv, device_id=device, device_id_type=MESH
        )

    def gather_rels(b):
        for e0 in range(0, edges, edge_tile):
            cols = slice(e0, e0 + edge_tile)
            hot = onehot(rel_ids[b : b + 1, cols], n_rel).astype(bf16)
            rel_hot[b, :, cols] = hot
            both = dot(rel_t[...], hot)
            rels_e[b, :, cols] = both[:width] + both[width:]

    def weigh(b, head, tail):
        head_t = jnp.concatenate(split(jnp.transpose(head)), axis=0)
        tail_hi, tail_lo = split(tail)
        tail_both = jnp.concatenate([tail_hi, tail_lo], axis=0)
        counts = jnp.sum(onehot(neg_ids[b : b + 1, :], rows).astype(f32), axis=1, keepdims=True)
        for e0 in range(0, edges, edge_tile):
            cols = slice(e0, e0 + edge_tile)
            both = dot(head_t, onehot(head_ids[b : b + 1, cols], rows).astype(bf16))
            heads = both[:rows] + both[rows:]
            heads_e[:, cols] = heads
            hi, lo = split(heads * rels_e[b, :, cols])
            hq_hi[:, cols] = hi
            hq_lo[:, cols] = lo
            both = dot(tail_both, hi)
            scores = both[:rows] + both[rows:] + dot(tail_hi, lo)
            tail_hot = onehot(tail_ids[b : b + 1, cols], rows)
            positive = jnp.sum(jnp.where(tail_hot, scores, 0.0), axis=0, keepdims=True)
            scores = jnp.where(counts > 0.0, scores, -3e38)
            ceiling = jnp.maximum(jnp.max(scores, axis=0, keepdims=True), positive)
            pos_exp = jnp.exp(positive - ceiling)
            neg_exp = jnp.exp(scores - ceiling) * counts
            inverse = 1.0 / (pos_exp + jnp.sum(neg_exp, axis=0, keepdims=True))
            weight = neg_exp * inverse + jnp.where(tail_hot, pos_exp * inverse - 1.0, 0.0)
            hi, lo = split(weight)
            wt_hi[:, cols] = hi
            wt_lo[:, cols] = lo

    def tail_gradient():
        return dot_nt(wt_hi[...], hq_hi[...]) + dot_nt(wt_hi[...], hq_lo[...]) + dot_nt(wt_lo[...], hq_hi[...])

    def pair_gradients(b, tail):
        tail_t_hi, tail_t_lo = split(jnp.transpose(tail))
        tail_t = jnp.concatenate([tail_t_hi, tail_t_lo], axis=0)
        for e0 in range(0, edges, edge_tile):
            cols = slice(e0, e0 + edge_tile)
            both = dot(tail_t, wt_hi[:, cols])
            pair = both[:width] + both[width:] + dot(tail_t_hi, wt_lo[:, cols])
            hi, lo = split(pair * rels_e[b, :, cols])
            by_head_hi[:, cols] = hi
            by_head_lo[:, cols] = lo
            hi, lo = split(pair * heads_e[:, cols])
            by_rel_hi[:, cols] = hi
            by_rel_lo[:, cols] = lo

    def head_gradient(b):
        hot = onehot(head_ids[b : b + 1, :], rows).astype(bf16)
        return dot_nt(hot, by_head_hi[...]) + dot_nt(hot, by_head_lo[...])

    loads[0].wait()
    rel_t[...] = jnp.concatenate(split(jnp.transpose(rel_ref[...])), axis=0)
    loads[1].wait()
    gather_rels(0)
    for load in loads[2:]:
        load.wait()
    weigh(0, head_ref[...], tail_ref[...])
    tail_new, tail_acc_new = adagrad(tail_ref[...], tail_acc_ref[...], tail_gradient())
    tail_send[:rows] = tail_new
    tail_send[rows:] = tail_acc_new
    pl.semaphore_wait(barrier, n_row + n_col - 2)
    tail_move = remote(tail_send, tail_in, move_send.at[0], move_recv.at[0], {"col": lax.rem(c + 1, n_col)})
    tail_move.start()
    pair_gradients(0, tail_ref[...])
    head_new, head_acc_new = adagrad(head_ref[...], head_acc_ref[...], head_gradient(0))
    head_send[:rows] = head_new
    head_send[rows:] = head_acc_new
    head_move = remote(head_send, head_in, move_send.at[1], move_recv.at[1], {"row": lax.rem(r + 1, n_row)})
    head_move.start()
    rel_one = dot_nt(rel_hot[0], by_rel_hi[...]) + dot_nt(rel_hot[0], by_rel_lo[...])
    grad[0] = rel_one[:, :half]
    grad[1] = rel_one[:, half:]
    gather_rels(1)
    head_move.wait()
    tail_move.wait()

    weigh(1, head_in[:rows], tail_in[:rows])
    pair_gradients(1, tail_in[:rows])

    stores = []

    def keep(src, dst, sem):
        stores.append(pltpu.make_async_copy(src, dst, sem))
        stores[-1].start()

    def x_start(i):
        return pl.multiple_of(lax.rem(x + i, n_x) * x_rows, x_rows)

    def z_start(i, k):
        return pl.multiple_of((lax.rem(x + i, n_x) * n_col + lax.rem(c + k, n_col)) * z_rows, z_rows)

    x_order = list(range(1, n_x)) + [0]
    z_order = list(range(1, n_col)) + [0]
    core_moves = {}
    for i in x_order:
        here = pl.ds(x_start(i), x_rows)
        part = dot_nt(rel_hot[1, here], by_rel_hi[...]) + dot_nt(rel_hot[1, here], by_rel_lo[...])
        grad[0, here] = grad[0, here] + part[:, :half]
        grad[1, here] = grad[1, here] + part[:, half:]
        core_moves[i] = remote(
            grad.at[1 - h, here], core_in.at[here], core_send.at[i], core_recv.at[i], {"row": sibling}
        )
        core_moves[i].start()

    x_moves = {}
    for i in x_order:
        core_moves[i].wait_recv()
        for k in z_order:
            here = pl.ds(z_start(i, k), z_rows)
            grad[h, here] = grad[h, here] + core_in[here]
            if i:
                slot = (i - 1) * n_col + k
                x_moves[i, k] = remote(
                    grad.at[h, here],
                    x_in.at[slot],
                    xs_send.at[slot],
                    xs_recv.at[slot],
                    {"row": lax.rem(x + i, n_x) * 2 + h},
                )
                x_moves[i, k].start()

    head_final, head_acc_final = adagrad(head_in[:rows], head_in[rows : rows + 1], head_gradient(1))
    head_out[...] = head_final
    head_acc_out[...] = head_acc_final[:1]
    keep(head_out, head_out_hbm, store_sems.at[0])
    keep(head_acc_out, head_acc_out_hbm, store_sems.at[1])
    tail_final, tail_acc_final = adagrad(tail_in[:rows], tail_in[rows : rows + 1], tail_gradient())
    tail_out[...] = tail_final
    tail_acc_out[...] = tail_acc_final[:1]
    keep(tail_out, tail_out_hbm, store_sems.at[2])
    keep(tail_acc_out, tail_acc_out_hbm, store_sems.at[3])
    for r0 in range(0, n_rel, 128):
        wide = jnp.broadcast_to(rel_acc_ref[:, r0 : r0 + 128], (128, 128))
        rel_acc_wide[r0 : r0 + 128] = jnp.transpose(wide)

    z_moves = {}
    for k in z_order:
        here = pl.ds(z_start(0, k), z_rows)
        value = grad[h, here]
        for i in range(1, n_x):
            x_moves[i, k].wait_recv()
            value = value + x_in[(i - 1) * n_col + k]
        grad[h, here] = value
        if k:
            z_moves[k] = remote(
                grad.at[h, here],
                z_in.at[k - 1],
                zs_send.at[k - 1],
                zs_recv.at[k - 1],
                {"col": lax.rem(c + k, n_col)},
            )
            z_moves[k].start()

    mine = pl.ds(z_start(0, 0), z_rows)
    value = grad[h, mine]
    for k in range(1, n_col):
        z_moves[k].wait_recv()
        value = value + z_in[k - 1]
    total[h, mine] = value

    gathers = []

    def spread(slot_x, slot_z, to_x):
        piece = total.at[h, pl.ds(z_start(slot_x, slot_z), z_rows)]
        if to_x:
            for i in range(1, n_x):
                slot = (i - 1) * n_col + slot_z
                gathers.append(
                    remote(piece, piece, xg_send.at[slot], xg_recv.at[slot], {"row": lax.rem(x + i, n_x) * 2 + h})
                )
                gathers[-1].start()
        slot = slot_x * n_col + slot_z
        gathers.append(remote(piece, piece, cg_send.at[slot], cg_recv.at[slot], {"row": sibling}))
        gathers[-1].start()

    piece = total.at[h, mine]
    for k in range(1, n_col):
        gathers.append(
            remote(piece, piece, zg_send.at[k - 1], zg_recv.at[k - 1], {"col": lax.rem(c + k, n_col)})
        )
        gathers[-1].start()
    spread(0, 0, True)

    def arrived(piece, sem):
        pltpu.make_async_copy(piece, piece, sem).wait()

    for k in range(1, n_col):
        from_z = n_col - k
        arrived(total.at[h, pl.ds(z_start(0, from_z), z_rows)], zg_recv.at[k - 1])
        spread(0, from_z, True)
    def finish(i, k):
        here = pl.ds(z_start(i, k), z_rows)
        arrived(total.at[1 - h, here], cg_recv.at[i * n_col + k])
        both = jnp.concatenate([total[0, here], total[1, here]], axis=1)
        mean = jnp.sum(both * both, axis=1, keepdims=True) * (1.0 / width)
        updated = rel_acc_wide[here] + mean
        rel_acc_wide[here] = updated
        rel_out[here] = rel_ref[here] - both * (learn_rate / jnp.sqrt(updated))[:, :1]
        keep(rel_out.at[here], rel_out_hbm.at[here], rel_store_sems.at[i * n_col + k])

    arrivals = [0] + list(range(n_col - 1, 0, -1))
    for k in arrivals:
        for i in range(1, n_x):
            from_x = n_x - i
            arrived(total.at[h, pl.ds(z_start(from_x, k), z_rows)], xg_recv.at[(i - 1) * n_col + k])
            spread(from_x, k, False)
        finish(0, k)
    for k in arrivals:
        for i in range(1, n_x):
            finish(n_x - i, k)
    for r0 in range(0, n_rel, 128):
        rel_acc_out[:, r0 : r0 + 128] = jnp.transpose(rel_acc_wide[r0 : r0 + 128])[:1]
    keep(rel_acc_out, rel_acc_out_hbm, store_sems.at[4])
    for move in stores:
        move.wait()
    for move in list(core_moves.values()) + list(x_moves.values()) + list(z_moves.values()) + gathers:
        move.wait_send()


def store(*refs):
    ins, outs, held = refs[:6], refs[6:12], refs[12:18]
    load_sems, store_sems = refs[18:]
    tiles = [(n, pl.ds(q, 128)) for n in (4, 0, 2) for q in range(0, ins[n].shape[0], 128)]
    tiles += [(n, slice(None)) for n in (5, 1, 3)]
    loads = [
        pltpu.make_async_copy(ins[n].at[part], held[n].at[part], load_sems.at[i])
        for i, (n, part) in enumerate(tiles)
    ]
    stores = [
        pltpu.make_async_copy(held[n].at[part], outs[n].at[part], store_sems.at[i])
        for i, (n, part) in enumerate(tiles)
    ]
    for load in loads:
        load.start()
    for load, move in zip(loads, stores):
        load.wait()
        move.start()
    for move in stores:
        move.wait()


def shards(
    n_row,
    n_col,
    head_table,
    head_accum,
    tail_table,
    tail_accum,
    relations,
    relation_accum,
    head_rows,
    tail_rows,
    relation_ids,
    negative_rows,
):
    rows, width = head_table.shape
    n_rel = relations.shape[0]
    buckets, edges = head_rows.shape[1:]
    n_x = n_row // 2
    half = width // 2
    z_rows = n_rel // (n_x * n_col)
    shape = jax.ShapeDtypeStruct
    dma = pltpu.SemaphoreType.DMA
    x_slots = max(1, (n_x - 1) * n_col)
    z_slots = max(1, n_col - 1)
    edge_piece = pltpu.VMEM((width, edges), bf16)
    moved = pltpu.VMEM((rows + 8, width), f32)
    outs = pl.pallas_call(
        functools.partial(kernel, n_row, n_col),
        out_shape=(
            shape((rows, width), f32),
            shape((1, rows), f32),
            shape((rows, width), f32),
            shape((1, rows), f32),
            shape((n_rel, width), f32),
            shape((1, n_rel), f32),
        ),
        in_specs=[pl.BlockSpec(memory_space=pltpu.HBM)] * 10,
        out_specs=(pl.BlockSpec(memory_space=pltpu.HBM),) * 6,
        scratch_shapes=[
            pltpu.VMEM((rows, width), f32),
            pltpu.VMEM((1, rows), f32),
            pltpu.VMEM((rows, width), f32),
            pltpu.VMEM((1, rows), f32),
            pltpu.VMEM((n_rel, width), f32),
            pltpu.VMEM((1, n_rel), f32),
            pltpu.VMEM((buckets, edges), jnp.int32),
            pltpu.VMEM((buckets, edges), jnp.int32),
            pltpu.VMEM((buckets, edges), jnp.int32),
            pltpu.VMEM(negative_rows.shape[1:], jnp.int32),
            dma((10,)),
            pltpu.VMEM((rows, width), f32),
            pltpu.VMEM((1, rows), f32),
            pltpu.VMEM((rows, width), f32),
            pltpu.VMEM((1, rows), f32),
            pltpu.VMEM((n_rel, width), f32),
            pltpu.VMEM((1, n_rel), f32),
            pltpu.VMEM((n_rel, 128), f32),
            dma((5,)),
            dma((n_x * n_col,)),
            pltpu.VMEM((2 * width, n_rel), bf16),
            pltpu.VMEM((buckets, n_rel, edges), bf16),
            pltpu.VMEM((buckets, width, edges), f32),
            pltpu.VMEM((width, edges), f32),
            edge_piece,
            edge_piece,
            pltpu.VMEM((rows, edges), bf16),
            pltpu.VMEM((rows, edges), bf16),
            edge_piece,
            edge_piece,
            edge_piece,
            edge_piece,
            moved,
            moved,
            moved,
            moved,
            pltpu.VMEM((2, n_rel, half), f32),
            pltpu.VMEM((n_rel, half), f32),
            pltpu.VMEM((x_slots, z_rows, half), f32),
            pltpu.VMEM((z_slots, z_rows, half), f32),
            pltpu.VMEM((2, n_rel, half), f32),
            dma((2,)),
            dma((2,)),
            dma((n_x,)),
            dma((n_x,)),
            dma((x_slots,)),
            dma((x_slots,)),
            dma((z_slots,)),
            dma((z_slots,)),
            dma((z_slots,)),
            dma((z_slots,)),
            dma((x_slots,)),
            dma((x_slots,)),
            dma((n_x * n_col,)),
            dma((n_x * n_col,)),
        ],
        compiler_params=pltpu.CompilerParams(
            collective_id=0, has_side_effects=True, vmem_limit_bytes=62 * 2**20
        ),
    )(
        head_table,
        head_accum.reshape(1, rows),
        tail_table,
        tail_accum.reshape(1, rows),
        relations,
        relation_accum.reshape(1, n_rel),
        head_rows[0],
        tail_rows[0],
        relation_ids[0],
        negative_rows[0],
    )
    outs = pl.pallas_call(
        store,
        out_shape=tuple(shape(out.shape, f32) for out in outs),
        in_specs=[pl.BlockSpec(memory_space=pltpu.HBM)] * 6,
        out_specs=(pl.BlockSpec(memory_space=pltpu.HBM),) * 6,
        scratch_shapes=[pltpu.VMEM(out.shape, f32) for out in outs]
        + [dma(((n_rel + 2 * rows) // 128 + 3,)), dma(((n_rel + 2 * rows) // 128 + 3,))],
        compiler_params=pltpu.CompilerParams(vmem_limit_bytes=62 * 2**20),
    )(*outs)
    return (outs[0], outs[1][0], outs[2], outs[3][0], outs[4], outs[5][0])


def solution(mesh):
    block = P(("groups", "row", "col"))
    return jax.shard_map(
        functools.partial(shards, mesh.shape["row"], mesh.shape["col"]),
        mesh=mesh,
        in_specs=(block, block, block, block, P("groups"), P("groups"), block, block, block, block),
        out_specs=(block, block, block, block, P("groups"), P("groups")),
        check_vma=False,
    )
```

```python
import functools

import jax
import jax.numpy as jnp
from jax import lax
from jax.experimental import pallas as pl
from jax.experimental.pallas import tpu as pltpu
from jax.sharding import PartitionSpec as P

learn_rate = 0.1
edge_tile = 256
f32 = jnp.float32
bf16 = jnp.bfloat16
MESH = pl.DeviceIdType.MESH


def split(value):
    high = value.astype(bf16)
    return high, (value - high.astype(f32)).astype(bf16)


def dot(a, b):
    return jnp.dot(a, b, preferred_element_type=f32)


def dot_nt(a, b):
    return lax.dot_general(a, b, (((1,), (1,)), ((), ())), preferred_element_type=f32)


def onehot(ids, count):
    rows = lax.broadcasted_iota(jnp.int32, (count, ids.shape[1]), 0)
    return rows == ids


def column(row):
    wide = jnp.broadcast_to(row, (128, row.shape[1]))
    return jnp.transpose(wide)[:, :1]


def as_row(col):
    wide = jnp.broadcast_to(col, (col.shape[0], 128))
    return jnp.transpose(wide)[:8]


def adagrad(weights, accum_row, gradient):
    width = gradient.shape[1]
    mean = jnp.sum(gradient * gradient, axis=1, keepdims=True) * (1.0 / width)
    updated = column(accum_row) + mean
    return weights - gradient * (learn_rate / jnp.sqrt(updated)), as_row(updated)


def kernel(
    n_row,
    n_col,
    head_hbm,
    head_acc_hbm,
    tail_hbm,
    tail_acc_hbm,
    rel_hbm,
    rel_acc_hbm,
    head_ids_hbm,
    tail_ids_hbm,
    rel_ids_hbm,
    neg_ids_hbm,
    head_out_hbm,
    head_acc_out_hbm,
    tail_out_hbm,
    tail_acc_out_hbm,
    rel_out_hbm,
    rel_acc_out_hbm,
    head_ref,
    head_acc_ref,
    tail_ref,
    tail_acc_ref,
    rel_ref,
    rel_acc_ref,
    head_ids,
    tail_ids,
    rel_ids,
    neg_ids,
    load_sems,
    head_out,
    head_acc_out,
    tail_out,
    tail_acc_out,
    rel_out,
    rel_acc_out,
    rel_acc_wide,
    store_sems,
    rel_store_sems,
    rel_t,
    rel_hot,
    rels_e,
    heads_e,
    hq_hi,
    hq_lo,
    wt_hi,
    wt_lo,
    by_head_hi,
    by_head_lo,
    by_rel_hi,
    by_rel_lo,
    head_send,
    tail_send,
    head_in,
    tail_in,
    grad,
    core_in,
    x_in,
    z_in,
    total,
    move_send,
    move_recv,
    core_send,
    core_recv,
    xs_send,
    xs_recv,
    zs_send,
    zs_recv,
    zg_send,
    zg_recv,
    xg_send,
    xg_recv,
    cg_send,
    cg_recv,
):
    n_x = n_row // 2
    rows, width = head_ref.shape
    n_rel = rel_ref.shape[0]
    edges = head_ids.shape[1]
    half = width // 2
    x_rows = n_rel // n_x
    z_rows = x_rows // n_col
    r = lax.axis_index("row")
    c = lax.axis_index("col")
    x = lax.div(r, 2)
    h = lax.rem(r, 2)
    sibling = x * 2 + (1 - h)

    pairs = (
        (rel_hbm, rel_ref),
        (rel_ids_hbm, rel_ids),
        (head_hbm, head_ref),
        (head_ids_hbm, head_ids),
        (tail_hbm, tail_ref),
        (tail_ids_hbm, tail_ids),
        (neg_ids_hbm, neg_ids),
        (tail_acc_hbm, tail_acc_ref),
        (head_acc_hbm, head_acc_ref),
        (rel_acc_hbm, rel_acc_ref),
    )
    loads = [pltpu.make_async_copy(src, dst, load_sems.at[n]) for n, (src, dst) in enumerate(pairs)]
    for load in loads:
        load.start()

    barrier = pltpu.get_barrier_semaphore()
    for k in range(1, n_row):
        pl.semaphore_signal(barrier, inc=1, device_id={"row": lax.rem(r + k, n_row)}, device_id_type=MESH)
    for k in range(1, n_col):
        pl.semaphore_signal(barrier, inc=1, device_id={"col": lax.rem(c + k, n_col)}, device_id_type=MESH)

    def remote(src, dst, send, recv, device):
        return pltpu.make_async_remote_copy(
            src_ref=src, dst_ref=dst, send_sem=send, recv_sem=recv, device_id=device, device_id_type=MESH
        )

    def gather_rels(b):
        for e0 in range(0, edges, edge_tile):
            cols = slice(e0, e0 + edge_tile)
            hot = onehot(rel_ids[b : b + 1, cols], n_rel).astype(bf16)
            rel_hot[b, :, cols] = hot
            both = dot(rel_t[...], hot)
            rels_e[b, :, cols] = both[:width] + both[width:]

    def project(b, head):
        head_t = jnp.concatenate(split(jnp.transpose(head)), axis=0)
        for e0 in range(0, edges, edge_tile):
            cols = slice(e0, e0 + edge_tile)
            both = dot(head_t, onehot(head_ids[b : b + 1, cols], rows).astype(bf16))
            heads = both[:rows] + both[rows:]
            heads_e[:, cols] = heads
            hi, lo = split(heads * rels_e[b, :, cols])
            hq_hi[:, cols] = hi
            hq_lo[:, cols] = lo

    def weigh(b, tail):
        tail_hi, tail_lo = split(tail)
        tail_both = jnp.concatenate([tail_hi, tail_lo], axis=0)
        counts = jnp.sum(onehot(neg_ids[b : b + 1, :], rows).astype(f32), axis=1, keepdims=True)
        for e0 in range(0, edges, edge_tile):
            cols = slice(e0, e0 + edge_tile)
            lo = hq_lo[:, cols]
            both = dot(tail_both, hq_hi[:, cols])
            scores = both[:rows] + both[rows:] + dot(tail_hi, lo)
            tail_hot = onehot(tail_ids[b : b + 1, cols], rows)
            positive = jnp.sum(jnp.where(tail_hot, scores, 0.0), axis=0, keepdims=True)
            scores = jnp.where(counts > 0.0, scores, -3e38)
            ceiling = jnp.maximum(jnp.max(scores, axis=0, keepdims=True), positive)
            pos_exp = jnp.exp(positive - ceiling)
            neg_exp = jnp.exp(scores - ceiling) * counts
            inverse = 1.0 / (pos_exp + jnp.sum(neg_exp, axis=0, keepdims=True))
            weight = neg_exp * inverse + jnp.where(tail_hot, pos_exp * inverse - 1.0, 0.0)
            hi, lo = split(weight)
            wt_hi[:, cols] = hi
            wt_lo[:, cols] = lo

    def tail_gradient():
        hi = wt_hi[...]
        return dot_nt(hi, hq_hi[...]) + dot_nt(hi, hq_lo[...]) + dot_nt(wt_lo[...], hq_hi[...])

    def pair_gradients(b, tail):
        tail_t_hi, tail_t_lo = split(jnp.transpose(tail))
        tail_t = jnp.concatenate([tail_t_hi, tail_t_lo], axis=0)
        for e0 in range(0, edges, edge_tile):
            cols = slice(e0, e0 + edge_tile)
            both = dot(tail_t, wt_hi[:, cols])
            pair = both[:width] + both[width:] + dot(tail_t_hi, wt_lo[:, cols])
            hi, lo = split(pair * rels_e[b, :, cols])
            by_head_hi[:, cols] = hi
            by_head_lo[:, cols] = lo
            hi, lo = split(pair * heads_e[:, cols])
            by_rel_hi[:, cols] = hi
            by_rel_lo[:, cols] = lo

    def pass_on(sent, held, slot, device):
        move = remote(sent, held, move_send.at[slot], move_recv.at[slot], device)
        move.start()
        return move

    def head_gradient(b):
        hot = onehot(head_ids[b : b + 1, :], rows).astype(bf16)
        return dot_nt(hot, by_head_hi[...]) + dot_nt(hot, by_head_lo[...])

    loads[0].wait()
    rel_t[...] = jnp.concatenate(split(jnp.transpose(rel_ref[...])), axis=0)
    loads[1].wait()
    gather_rels(0)
    for load in loads[2:]:
        load.wait()
    project(0, head_ref[...])
    weigh(0, tail_ref[...])
    tail_new, tail_acc_new = adagrad(tail_ref[...], tail_acc_ref[...], tail_gradient())
    tail_send[:rows] = tail_new
    tail_send[rows:] = tail_acc_new
    pl.semaphore_wait(barrier, n_row + n_col - 2)
    tail_move = pass_on(tail_send, tail_in, 0, {"col": lax.rem(c + 1, n_col)})
    pair_gradients(0, tail_ref[...])
    head_new, head_acc_new = adagrad(head_ref[...], head_acc_ref[...], head_gradient(0))
    head_send[:rows] = head_new
    head_send[rows:] = head_acc_new
    head_move = pass_on(head_send, head_in, 1, {"row": lax.rem(r + 1, n_row)})
    rel_one = dot_nt(rel_hot[0], by_rel_hi[...]) + dot_nt(rel_hot[0], by_rel_lo[...])
    grad[0] = rel_one[:, :half]
    grad[1] = rel_one[:, half:]
    gather_rels(1)
    head_move.wait()
    project(1, head_in[:rows])
    tail_move.wait()
    weigh(1, tail_in[:rows])
    pair_gradients(1, tail_in[:rows])

    stores = []

    def keep(src, dst, sem):
        stores.append(pltpu.make_async_copy(src, dst, sem))
        stores[-1].start()

    def x_start(i):
        return pl.multiple_of(lax.rem(x + i, n_x) * x_rows, x_rows)

    def z_start(i, k):
        return pl.multiple_of((lax.rem(x + i, n_x) * n_col + lax.rem(c + k, n_col)) * z_rows, z_rows)

    x_order = list(range(1, n_x)) + [0]
    z_order = list(range(1, n_col)) + [0]
    core_moves = {}
    for i in x_order:
        here = pl.ds(x_start(i), x_rows)
        part = dot_nt(rel_hot[1, here], by_rel_hi[...]) + dot_nt(rel_hot[1, here], by_rel_lo[...])
        grad[0, here] = grad[0, here] + part[:, :half]
        grad[1, here] = grad[1, here] + part[:, half:]
        core_moves[i] = remote(
            grad.at[1 - h, here], core_in.at[here], core_send.at[i], core_recv.at[i], {"row": sibling}
        )
        core_moves[i].start()

    x_moves = {}
    for i in x_order:
        core_moves[i].wait_recv()
        for k in z_order:
            here = pl.ds(z_start(i, k), z_rows)
            grad[h, here] = grad[h, here] + core_in[here]
            if i:
                slot = (i - 1) * n_col + k
                x_moves[i, k] = remote(
                    grad.at[h, here],
                    x_in.at[slot],
                    xs_send.at[slot],
                    xs_recv.at[slot],
                    {"row": lax.rem(x + i, n_x) * 2 + h},
                )
                x_moves[i, k].start()

    head_final, head_acc_final = adagrad(head_in[:rows], head_in[rows : rows + 1], head_gradient(1))
    head_out[...] = head_final
    head_acc_out[...] = head_acc_final[:1]
    keep(head_out, head_out_hbm, store_sems.at[0])
    keep(head_acc_out, head_acc_out_hbm, store_sems.at[1])
    tail_final, tail_acc_final = adagrad(tail_in[:rows], tail_in[rows : rows + 1], tail_gradient())
    tail_out[...] = tail_final
    tail_acc_out[...] = tail_acc_final[:1]
    keep(tail_out, tail_out_hbm, store_sems.at[2])
    keep(tail_acc_out, tail_acc_out_hbm, store_sems.at[3])
    for r0 in range(0, n_rel, 128):
        wide = jnp.broadcast_to(rel_acc_ref[:, r0 : r0 + 128], (128, 128))
        rel_acc_wide[r0 : r0 + 128] = jnp.transpose(wide)

    z_moves = {}
    for k in z_order:
        here = pl.ds(z_start(0, k), z_rows)
        value = grad[h, here]
        for i in range(1, n_x):
            x_moves[i, k].wait_recv()
            value = value + x_in[(i - 1) * n_col + k]
        grad[h, here] = value
        if k:
            z_moves[k] = remote(
                grad.at[h, here],
                z_in.at[k - 1],
                zs_send.at[k - 1],
                zs_recv.at[k - 1],
                {"col": lax.rem(c + k, n_col)},
            )
            z_moves[k].start()

    mine = pl.ds(z_start(0, 0), z_rows)
    value = grad[h, mine]
    for k in range(1, n_col):
        z_moves[k].wait_recv()
        value = value + z_in[k - 1]
    total[h, mine] = value

    gathers = []

    def spread(slot_x, slot_z, to_x):
        piece = total.at[h, pl.ds(z_start(slot_x, slot_z), z_rows)]
        if to_x:
            for i in range(1, n_x):
                slot = (i - 1) * n_col + slot_z
                gathers.append(
                    remote(piece, piece, xg_send.at[slot], xg_recv.at[slot], {"row": lax.rem(x + i, n_x) * 2 + h})
                )
                gathers[-1].start()
        slot = slot_x * n_col + slot_z
        gathers.append(remote(piece, piece, cg_send.at[slot], cg_recv.at[slot], {"row": sibling}))
        gathers[-1].start()

    piece = total.at[h, mine]
    for k in range(1, n_col):
        gathers.append(
            remote(piece, piece, zg_send.at[k - 1], zg_recv.at[k - 1], {"col": lax.rem(c + k, n_col)})
        )
        gathers[-1].start()
    spread(0, 0, True)

    def arrived(piece, sem):
        pltpu.make_async_copy(piece, piece, sem).wait()

    for k in range(1, n_col):
        from_z = n_col - k
        arrived(total.at[h, pl.ds(z_start(0, from_z), z_rows)], zg_recv.at[k - 1])
        spread(0, from_z, True)
    def finish(i, k):
        here = pl.ds(z_start(i, k), z_rows)
        arrived(total.at[1 - h, here], cg_recv.at[i * n_col + k])
        both = jnp.concatenate([total[0, here], total[1, here]], axis=1)
        mean = jnp.sum(both * both, axis=1, keepdims=True) * (1.0 / width)
        updated = rel_acc_wide[here] + mean
        rel_acc_wide[here] = updated
        rel_out[here] = rel_ref[here] - both * (learn_rate / jnp.sqrt(updated))[:, :1]
        keep(rel_out.at[here], rel_out_hbm.at[here], rel_store_sems.at[i * n_col + k])

    arrivals = [0] + list(range(n_col - 1, 0, -1))
    for k in arrivals:
        for i in range(1, n_x):
            from_x = n_x - i
            arrived(total.at[h, pl.ds(z_start(from_x, k), z_rows)], xg_recv.at[(i - 1) * n_col + k])
            spread(from_x, k, False)
        finish(0, k)
    for k in arrivals:
        for i in range(1, n_x):
            finish(n_x - i, k)
    for r0 in range(0, n_rel, 128):
        rel_acc_out[:, r0 : r0 + 128] = jnp.transpose(rel_acc_wide[r0 : r0 + 128])[:1]
    keep(rel_acc_out, rel_acc_out_hbm, store_sems.at[4])
    for move in stores:
        move.wait()
    for move in list(core_moves.values()) + list(x_moves.values()) + list(z_moves.values()) + gathers:
        move.wait_send()


def store(*refs):
    ins, outs, held = refs[:6], refs[6:12], refs[12:18]
    load_sems, store_sems = refs[18:]
    tiles = [(n, pl.ds(q, 128)) for n in (4, 0, 2) for q in range(0, ins[n].shape[0], 128)]
    tiles += [(n, slice(None)) for n in (5, 1, 3)]
    loads = [
        pltpu.make_async_copy(ins[n].at[part], held[n].at[part], load_sems.at[i])
        for i, (n, part) in enumerate(tiles)
    ]
    stores = [
        pltpu.make_async_copy(held[n].at[part], outs[n].at[part], store_sems.at[i])
        for i, (n, part) in enumerate(tiles)
    ]
    for load in loads:
        load.start()
    for load, move in zip(loads, stores):
        load.wait()
        move.start()
    for move in stores:
        move.wait()


def shards(
    n_row,
    n_col,
    head_table,
    head_accum,
    tail_table,
    tail_accum,
    relations,
    relation_accum,
    head_rows,
    tail_rows,
    relation_ids,
    negative_rows,
):
    rows, width = head_table.shape
    n_rel = relations.shape[0]
    buckets, edges = head_rows.shape[1:]
    n_x = n_row // 2
    half = width // 2
    z_rows = n_rel // (n_x * n_col)
    shape = jax.ShapeDtypeStruct
    dma = pltpu.SemaphoreType.DMA
    x_slots = max(1, (n_x - 1) * n_col)
    z_slots = max(1, n_col - 1)
    edge_piece = pltpu.VMEM((width, edges), bf16)
    moved = pltpu.VMEM((rows + 8, width), f32)
    outs = pl.pallas_call(
        functools.partial(kernel, n_row, n_col),
        out_shape=(
            shape((rows, width), f32),
            shape((1, rows), f32),
            shape((rows, width), f32),
            shape((1, rows), f32),
            shape((n_rel, width), f32),
            shape((1, n_rel), f32),
        ),
        in_specs=[pl.BlockSpec(memory_space=pltpu.HBM)] * 10,
        out_specs=(pl.BlockSpec(memory_space=pltpu.HBM),) * 6,
        scratch_shapes=[
            pltpu.VMEM((rows, width), f32),
            pltpu.VMEM((1, rows), f32),
            pltpu.VMEM((rows, width), f32),
            pltpu.VMEM((1, rows), f32),
            pltpu.VMEM((n_rel, width), f32),
            pltpu.VMEM((1, n_rel), f32),
            pltpu.VMEM((buckets, edges), jnp.int32),
            pltpu.VMEM((buckets, edges), jnp.int32),
            pltpu.VMEM((buckets, edges), jnp.int32),
            pltpu.VMEM(negative_rows.shape[1:], jnp.int32),
            dma((10,)),
            pltpu.VMEM((rows, width), f32),
            pltpu.VMEM((1, rows), f32),
            pltpu.VMEM((rows, width), f32),
            pltpu.VMEM((1, rows), f32),
            pltpu.VMEM((n_rel, width), f32),
            pltpu.VMEM((1, n_rel), f32),
            pltpu.VMEM((n_rel, 128), f32),
            dma((5,)),
            dma((n_x * n_col,)),
            pltpu.VMEM((2 * width, n_rel), bf16),
            pltpu.VMEM((buckets, n_rel, edges), bf16),
            pltpu.VMEM((buckets, width, edges), f32),
            pltpu.VMEM((width, edges), f32),
            edge_piece,
            edge_piece,
            pltpu.VMEM((rows, edges), bf16),
            pltpu.VMEM((rows, edges), bf16),
            edge_piece,
            edge_piece,
            edge_piece,
            edge_piece,
            moved,
            moved,
            moved,
            moved,
            pltpu.VMEM((2, n_rel, half), f32),
            pltpu.VMEM((n_rel, half), f32),
            pltpu.VMEM((x_slots, z_rows, half), f32),
            pltpu.VMEM((z_slots, z_rows, half), f32),
            pltpu.VMEM((2, n_rel, half), f32),
            dma((2,)),
            dma((2,)),
            dma((n_x,)),
            dma((n_x,)),
            dma((x_slots,)),
            dma((x_slots,)),
            dma((z_slots,)),
            dma((z_slots,)),
            dma((z_slots,)),
            dma((z_slots,)),
            dma((x_slots,)),
            dma((x_slots,)),
            dma((n_x * n_col,)),
            dma((n_x * n_col,)),
        ],
        compiler_params=pltpu.CompilerParams(
            collective_id=0, has_side_effects=True, vmem_limit_bytes=62 * 2**20
        ),
    )(
        head_table,
        head_accum.reshape(1, rows),
        tail_table,
        tail_accum.reshape(1, rows),
        relations,
        relation_accum.reshape(1, n_rel),
        head_rows[0],
        tail_rows[0],
        relation_ids[0],
        negative_rows[0],
    )
    outs = pl.pallas_call(
        store,
        out_shape=tuple(shape(out.shape, f32) for out in outs),
        in_specs=[pl.BlockSpec(memory_space=pltpu.HBM)] * 6,
        out_specs=(pl.BlockSpec(memory_space=pltpu.HBM),) * 6,
        scratch_shapes=[pltpu.VMEM(out.shape, f32) for out in outs]
        + [dma(((n_rel + 2 * rows) // 128 + 3,)), dma(((n_rel + 2 * rows) // 128 + 3,))],
        compiler_params=pltpu.CompilerParams(vmem_limit_bytes=62 * 2**20),
    )(*outs)
    return (outs[0], outs[1][0], outs[2], outs[3][0], outs[4], outs[5][0])


def solution(mesh):
    block = P(("groups", "row", "col"))
    return jax.shard_map(
        functools.partial(shards, mesh.shape["row"], mesh.shape["col"]),
        mesh=mesh,
        in_specs=(block, block, block, block, P("groups"), P("groups"), block, block, block, block),
        out_specs=(block, block, block, block, P("groups"), P("groups")),
        check_vma=False,
    )
```
